128 devices in a mesh: obs: 8 (over x, z_lo), par: 16 (over z_hi, y, core).
Axes of the slice: x: 4, y: 4, z: 4 (z_hi: 2, z_lo: 2; z = z_hi * 2 + z_lo), core: 2. Of those that a mesh axis runs over, the one named last changes fastest.
Arguments:
- jacobian: float32 [3584, 10240], P('obs', 'par'), may hold values from -0.09375 to 0.09375
- obs_group: int32 [3584], P('obs'), may hold values from 0 to 2
- group_weight: float32 [3], replicated, may hold values from 0.5 to 4
- misfit: float32 [3584], P('obs'), may hold values from -6 to 6
Outputs:
- normal_matrix: float32 [10240, 10240], P('obs', 'par')
- gradient: float32 [10240], P('par')
The draws below stay inside these ranges and needn't reach their ends.
All inputs are finite; a program needn't handle non-finite values.
Results may differ from the reference program's by a relative error of at most 0.00013.
Values sent between devices are 32-bit elements; how exact they have to be, the bound alone decides.
No kernel may reach another device: no remote copies, remote signals or barrier semaphores. Data moves between devices by JAX's collectives and lax.ppermute only.
A program may use at most 128 MiB of HBM per device.

```python
import math
import jax
import jax.numpy as jnp
from jax import lax

P_SIZE = 10240
GROUPS = 3
ROWS = 3584


def set_ends(values, rng, low, largest):
    shape = values.shape
    index_at = [jax.random.randint(jax.random.fold_in(rng, axis), (), 0, shape[axis]) for axis in range(len(shape))]
    values = values.at[tuple(index_at)].set(low)
    longest = shape.index(max(shape))
    index_at[longest] = (index_at[longest] + 1) % shape[longest]
    return values.at[tuple(index_at)].set(largest)


def block_levels(key, extent, cuts, least, top_value):
    gain, own = 1.0, jax.random.fold_in(key, 6)
    for position, shards_of in cuts:
        steps = jnp.exp(jax.random.uniform(jax.random.fold_in(own, position), (shards_of,), jnp.float32, least / len(cuts), top_value / len(cuts)))
        gain = gain * jnp.repeat(steps, extent[position] // shards_of).reshape([-1 if axis == position else 1 for axis in range(len(extent))])
    return gain


def scatter_about(own_key, extent, scale, bound, cuts=(), dtype=jnp.bfloat16):
    entries = jax.random.normal(own_key, extent, jnp.float32) * scale
    if len(cuts) > 0:
        entries = block_levels(own_key, extent, cuts, -0.22, 0.18) * entries
    return jnp.clip(entries, min=-bound, max=bound).astype(dtype)


def setup_inputs(seed: int = 0) -> dict:
    seeds = jax.random.split(jax.random.key(seed), 5)
    return {
        "jacobian": scatter_about(seeds[0], (ROWS, P_SIZE), ROWS ** -0.5, 0.09375, ((0, 8), (1, 16)), jnp.float32),
        "obs_group": set_ends(jax.random.randint(seeds[1], (ROWS,), 0, GROUPS), jax.random.fold_in(seeds[1], 1), 0, GROUPS - 1).astype(jnp.int32),
        "group_weight": jnp.clip(jnp.exp(jax.random.uniform(seeds[2], (GROUPS,), jnp.float32, math.log(0.5), math.log(4.0))), 0.5, 4.0),
        "misfit": scatter_about(seeds[3], (ROWS,), 1.0, 6.0, ((0, 8),), jnp.float32),
    }


def reference(jacobian, obs_group, group_weight, misfit):
    row_weight = group_weight[obs_group]
    weighted = jacobian * row_weight[:, None]
    normal_matrix = lax.dot_general(jacobian, weighted, (((0,), (0,)), ((), ())), precision=lax.Precision.HIGHEST, preferred_element_type=jnp.float32)
    gradient = jnp.dot(row_weight * misfit, jacobian, precision=lax.Precision.HIGHEST, preferred_element_type=jnp.float32)
    return normal_matrix, gradient
```

```python
import jax
import jax.numpy as jnp
from jax import lax
from jax.sharding import PartitionSpec as P

AXES = ("obs", "par")
X, ZLO, ZHI, Y, CORE = 4, 2, 2, 4, 2
PHASES = (96, 160, 192)


def linear(x, zlo, zhi, y, core):
    return (((x * ZLO + zlo) * ZHI + zhi) * Y + y) * CORE + core


def send(value, target):
    pairs = []
    for x in range(X):
        for zlo in range(ZLO):
            for zhi in range(ZHI):
                for y in range(Y):
                    for core in range(CORE):
                        there = target(x, zlo, zhi, y, core)
                        pairs.append((linear(x, zlo, zhi, y, core), linear(*there)))
    return lax.ppermute(value, AXES, pairs)


def along_x(step):
    return lambda x, zlo, zhi, y, core: ((x + step) % X, zlo, zhi, y, core)


def flip_x(mask):
    return lambda x, zlo, zhi, y, core: (x ^ mask, zlo, zhi, y, core)


def flip_zlo(x, zlo, zhi, y, core):
    return x, zlo ^ 1, zhi, y, core


def flip_zhi(x, zlo, zhi, y, core):
    return x, zlo, zhi ^ 1, y, core


def flip_core(x, zlo, zhi, y, core):
    return x, zlo, zhi, y, core ^ 1


def both_ways_y(x, zlo, zhi, y, core):
    return x, zlo, zhi, (y + (1 if core == 0 else -1)) % Y, core


def to_output_rows(x, zlo, zhi, y, core):
    return zhi * 2 + y // 2, y % 2, zhi ^ zlo ^ (y % 2), x, core


def pair(own, other, own_second, axis):
    return jnp.where(
        own_second,
        jnp.concatenate([other, own], axis),
        jnp.concatenate([own, other], axis),
    )


def body(jacobian, obs_group, group_weight, misfit):
    obs, par = lax.axis_index("obs"), lax.axis_index("par")
    x, zlo = obs // ZLO, obs % ZLO
    zhi, y, core = par // (Y * CORE), (par // CORE) % Y, par % CORE
    levels = jnp.arange(group_weight.shape[0], dtype=jnp.int32)
    onehot = (obs_group[:, None] == levels[None, :]).astype(jnp.float32)
    weight_row = jnp.sum(onehot * group_weight[None, :], axis=1)
    weighted = jacobian * weight_row[:, None]

    gradient = jnp.sum(jacobian * (weight_row * misfit)[:, None], axis=0)
    for target in (flip_zlo, flip_x(1), flip_x(2)):
        gradient = gradient + send(gradient, target)

    second = (zlo ^ zhi ^ (x // 2)) == 1
    columns = jacobian.shape[1]
    total = None
    low = 0
    for rows in PHASES:
        mine = jacobian[low : low + rows]
        here = weighted[low : low + rows]
        low += rows
        here = send(here, to_output_rows)
        here = pair(here, send(here, flip_core), core == 1, 1)[None]
        far = send(lax.dynamic_slice(here, (0, 0, core * columns), (1, rows, columns)), flip_zhi)
        far = pair(far, send(far, flip_core), core == 1, 2)
        here = pair(here, far, second, 0)
        left = jnp.zeros((Y, 2, rows, 2 * columns), jnp.float32)
        left = lax.dynamic_update_slice(left, here[None], (y, 0, 0, 0))
        got = send(here, both_ways_y)
        passed = send(lax.dynamic_slice(got, (core, 0, 0), (1, rows, 2 * columns)), both_ways_y)
        ahead = (y + 1) % Y
        behind = (y + Y - 1) % Y
        across = (y + 2) % Y
        left = lax.dynamic_update_slice(left, got[None], (jnp.where(core == 0, behind, ahead), 0, 0, 0))
        left = lax.dynamic_update_slice(
            left, send(got, flip_core)[None], (jnp.where(core == 0, ahead, behind), 0, 0, 0)
        )
        left = lax.dynamic_update_slice(left, passed[None], (across, core, 0, 0))
        left = lax.dynamic_update_slice(left, send(passed, flip_core)[None], (across, 1 - core, 0, 0))
        mine = pair(mine[None], send(mine[None], flip_zlo), zlo == 1, 0)
        right = jnp.zeros((X, 2, rows, columns), jnp.float32)
        right = lax.dynamic_update_slice(right, mine[None], (x, 0, 0, 0))
        behind = send(mine, along_x(1))
        ahead = send(mine, along_x(-1))
        right = lax.dynamic_update_slice(right, behind[None], ((x + X - 1) % X, 0, 0, 0))
        right = lax.dynamic_update_slice(right, ahead[None], ((x + 1) % X, 0, 0, 0))
        right = lax.dynamic_update_slice(right, send(behind[:1], along_x(1))[None], ((x + 2) % X, 0, 0, 0))
        right = lax.dynamic_update_slice(right, send(ahead[1:], along_x(-1))[None], ((x + 2) % X, 1, 0, 0))
        term = lax.dot_general(
            left.reshape(-1, 2 * columns),
            right.reshape(-1, columns),
            (((0,), (0,)), ((), ())),
            precision=lax.Precision.HIGH,
            preferred_element_type=jnp.float32,
        )
        total = term if total is None else total + term
    return total, gradient


def solution(mesh):
    return jax.shard_map(
        body,
        mesh=mesh,
        in_specs=(P("obs", "par"), P("obs"), P(), P("obs")),
        out_specs=(P("obs", "par"), P("par")),
        check_vma=False,
    )
```

```python
import functools

import jax
import jax.numpy as jnp
from jax import lax
from jax.experimental import pallas as pl
from jax.experimental.pallas import tpu as pltpu
from jax.sharding import Mesh, PartitionSpec as P

NAMES = ("x", "zlo", "zhi", "y", "core")
SIZES = (4, 2, 2, 4, 2)
X, ZLO, ZHI, Y, CORE = SIZES
PHASES = (96, 128)
TILE = 8
ORDER = (
    ('X1',),
    ('T1a',),
    ('T2a', 'T1a'),
    ('T1b', 'T1a'),
    ('Z', 'X1'),
    ('NOa', 'T2a'),
    ('ZHa', 'T2a'),
    ('T2b', 'T1b'),
    ('X2', 'X1'),
    ('FOa', 'NOa'),
    ('NPa', 'ZHa'),
    ('ZHb', 'T2b'),
    ('NOb', 'T2b'),
    ('V1', 'Z'),
    ('FPa', 'NPa', 'FOa'),
    ('FOb', 'NOb', 'FPa', 'X2'),
    ('NPb', 'ZHb', 'V1'),
    ('V2', 'V1'),
    ('FPb', 'NPb', 'FOb'),
)


def linear(x, zlo, zhi, y, core):
    return (((x * ZLO + zlo) * ZHI + zhi) * Y + y) * CORE + core


def send(value, target):
    pairs = []
    for x in range(X):
        for zlo in range(ZLO):
            for zhi in range(ZHI):
                for y in range(Y):
                    for core in range(CORE):
                        there = target(x, zlo, zhi, y, core)
                        pairs.append((linear(x, zlo, zhi, y, core), linear(*there)))
    return lax.ppermute(value, NAMES, pairs)


NEAR, FAR = (1, 3), (3, 1)


def flip_x(masks):
    return lambda x, zlo, zhi, y, core: (x ^ masks[core], zlo, zhi, y, core)


def flip_y(masks):
    return lambda x, zlo, zhi, y, core: (x, zlo, zhi, y ^ masks[core], core)


def flip_zlo(x, zlo, zhi, y, core):
    return x, zlo ^ 1, zhi, y, core


def flip_zhi(x, zlo, zhi, y, core):
    return x, zlo, zhi ^ 1, y, core


def flip_core(x, zlo, zhi, y, core):
    return x, zlo, zhi, y, core ^ 1


def spread_yz(x, zlo, zhi, y, core):
    y = y ^ (2 * ((x & 1) ^ core) + zlo)
    return x, zlo ^ (y & 1), zhi ^ (x >> 1) ^ core, y, core


def spread_x(x, zlo, zhi, y, core):
    return x ^ (2 * (zhi ^ core) + ((y >> 1) ^ core)), zlo, zhi, y, core


def in_two(value):
    high = value.astype(jnp.bfloat16)
    return high, (value - high.astype(jnp.float32)).astype(jnp.bfloat16)


def dot(a, b):
    return lax.dot_general(a, b, (((0,), (0,)), ((), ())), preferred_element_type=jnp.float32)


def contract(left, right):
    left_high, left_low = in_two(left.reshape(-1, left.shape[-1]))
    right_high, right_low = in_two(right.reshape(-1, right.shape[-1]))
    return dot(left_high, right_high) + (dot(left_low, right_high) + dot(left_high, right_low))


def accumulate(low, steps, pick_ref, *refs):
    lefts, rights = refs[: len(low)], refs[len(low) : len(low) + ZLO]
    out_ref, rest = refs[-1], refs[len(low) + ZLO : -1]
    step = pl.program_id(1)

    @pl.when(step == 0)
    def _():
        out_ref[...] = rest[0][...] if rest else jnp.zeros_like(out_ref)

    for which in range(ZLO):
        if steps[which]:

            @pl.when(step // 2 == which if all(steps) else step >= 0)
            def _():
                out_ref[0] += functools.reduce(
                    lambda p, q: p + q,
                    [
                        contract(lefts[k][0], rights[which][:, low[k] : low[k] + lefts[k].shape[2]])
                        for k in steps[which]
                    ],
                )


def product(lefts, low, panels, sides, total, steps):
    wide = panels[0].shape[-1]
    columns = wide // CORE
    count = panels[0].shape[1] // TILE * TILE
    n = sides.shape[0]
    block = pl.BlockSpec((1, wide, columns), lambda s, i, pick: (pick[s], 0, 0))
    rows = sum(left.shape[2] for left in lefts)
    both = all(steps)
    alone = 0 if steps[0] else 1

    def left_spec(k, left):
        always = [which for which in range(ZLO) if k in steps[which]]
        if len(always) == 2:
            index = lambda s, i, pick: (i // 2, i % 2, 0, 0)
        else:
            index = lambda s, i, pick: (always[0], i % 2, 0, 0)
        return pl.BlockSpec((1, 2, left.shape[2], wide), index)

    def right_spec(which):
        if not both:
            index = (lambda s, i, pick: (i, 0, pick[s])) if which == alone else (lambda s, i, pick: (0, 0, 0))
        elif which == 0:
            index = lambda s, i, pick: (jnp.minimum(i, 1), 0, pick[s])
        else:
            index = lambda s, i, pick: (jnp.maximum(i - 2, 0), 0, pick[s])
        return pl.BlockSpec((2, count, columns), index)

    return pl.pallas_call(
        functools.partial(accumulate, low, steps),
        grid_spec=pltpu.PrefetchScalarGridSpec(
            num_scalar_prefetch=1,
            grid=(n, 4 if both else 2),
            in_specs=[left_spec(k, left) for k, left in enumerate(lefts)]
            + [right_spec(which) for which in range(ZLO)]
            + ([] if total is None else [block]),
            out_specs=block if n > 1 else pl.BlockSpec((1, wide, columns), lambda s, i, pick: (0, 0, 0)),
        ),
        out_shape=jax.ShapeDtypeStruct((n, wide, columns), jnp.float32),
        compiler_params=pltpu.CompilerParams(vmem_limit_bytes=56 * 2**20),
        cost_estimate=pl.CostEstimate(
            flops=6 * n * ZLO * X * rows * wide * columns,
            bytes_accessed=4 * n * ZLO * X * (rows + count) * wide,
            transcendentals=0,
        ),
    )(sides, *lefts, *panels, *(() if total is None else (total,)))


def body(jacobian, obs_group, group_weight, misfit):
    x, zlo, zhi, y, core = (lax.axis_index(name) for name in NAMES)
    count, columns = jacobian.shape[0] // CORE, jacobian.shape[1]
    levels = jnp.arange(group_weight.shape[0], dtype=jnp.int32)
    onehot = (obs_group[:, None] == levels[None, :]).astype(jnp.float32)
    weight_row = jnp.sum(onehot * group_weight[None, :], axis=1)
    names = "abcd"[: len(PHASES)]
    low = {p: sum(PHASES[: names.index(p)]) for p in names}
    size = dict(zip(names, PHASES))
    got = {}

    kept = lax.dynamic_slice_in_dim(jacobian, core * count, count, 0)
    given = lax.dynamic_slice_in_dim(jacobian, (1 - core) * count, count, 0)
    taken = send(given, flip_core)
    mine = jnp.where(
        core == 0, jnp.concatenate([kept, taken], 1), jnp.concatenate([taken, kept], 1)
    )
    row_weight = lax.dynamic_slice_in_dim(weight_row, core * count, count, 0)[:, None]
    row_misfit = lax.dynamic_slice_in_dim(misfit, core * count, count, 0)[:, None]
    local = jnp.sum(mine * (row_weight * row_misfit), axis=0)

    def weighted(p):
        rows = slice(low[p], low[p] + size[p])
        return mine[rows] * row_weight[rows]

    def wide():
        return jnp.concatenate([mine, jnp.broadcast_to(local[None], (TILE, 2 * columns))], 0)

    def partner():
        return got["Z"].at[count:].add(local[None])

    def both(*names):
        return jnp.concatenate([got[n] if got[n].ndim == 3 else got[n][None] for n in names], 0)

    rings = {"N": flip_y(NEAR), "F": flip_y(FAR)}
    moves = {
        "X1": (lambda: mine, flip_x(NEAR)),
        "X2": (lambda: jnp.stack([mine, got["X1"]]), flip_x(FAR)),
        "Z": (wide, flip_zlo),
        "V1": (partner, flip_x(NEAR)),
        "V2": (lambda: jnp.stack([partner(), got["V1"]]), flip_x(FAR)),
    }
    for p in size:
        moves["T1" + p] = (functools.partial(weighted, p), spread_yz)
        moves["T2" + p] = (lambda p=p: got["T1" + p], spread_x)
        moves["ZH" + p] = (lambda p=p: got["T2" + p], flip_zhi)
        moves["NO" + p] = (lambda p=p: got["T2" + p], rings["N"])
        moves["FO" + p] = (lambda p=p: both("T2" + p, "NO" + p), rings["F"])
        moves["NP" + p] = (lambda p=p: got["ZH" + p], rings["N"])
        moves["FP" + p] = (lambda p=p: both("ZH" + p, "NP" + p), rings["F"])
        moves["NC" + p] = (lambda p=p: both("T2" + p, "ZH" + p), rings["N"])
        moves["FC" + p] = (lambda p=p: both("T2" + p, "ZH" + p, "NC" + p), rings["F"])

    token = jnp.zeros((TILE, 128), jnp.float32)
    for name, *after in ORDER:
        value = moves[name][0]()
        if after:
            held = [got[a] for a in after]
            value, token, *held = lax.optimization_barrier((value, token, *held))
            got.update(zip(after, held))
        got[name] = send(value, moves[name][1])

    near = jnp.where(core == 0, NEAR[0], NEAR[1])
    far = jnp.where(core == 0, FAR[0], FAR[1])

    def panel(first, one, two):
        out = jnp.zeros((X, *first.shape), jnp.float32)
        for at, block in ((0, first), (near, one), (far, two[0]), (near ^ far, two[1])):
            out = lax.dynamic_update_slice(out, block[None], (at, 0, 0))
        return out

    panels = (
        panel(mine, got["X1"], got["X2"]),
        panel(partner(), got["V1"], got["V2"]),
    )
    slope = jnp.sum(panels[1][:, count], axis=0)
    gradient = lax.dynamic_slice_in_dim(slope, core * columns, columns, 0) + send(
        lax.dynamic_slice_in_dim(slope, (1 - core) * columns, columns, 0), flip_core
    )

    def collect(p):
        out = jnp.zeros((ZLO, X, size[p], 2 * columns), jnp.float32)
        for other in range(ZHI):
            if "NC" + p in got:
                k = other
                pieces = ((0, got["ZH" + p] if other else got["T2" + p]), (near, got["NC" + p][k]))
                pieces += ((far, got["FC" + p][k]), (near ^ far, got["FC" + p][2 + k]))
            else:
                first, one, two = (got[n + p] for n in (("ZH", "NP", "FP") if other else ("T2", "NO", "FO")))
                pieces = ((0, first), (near, one), (far, two[0]), (near ^ far, two[1]))
            for step, block in pieces:
                there = y ^ step
                at = 2 * (zhi ^ other ^ core) + ((there >> 1) ^ core)
                out = lax.dynamic_update_slice(out, block[None, None], (there & 1, at, 0, 0))
        return out

    sides = jnp.stack([1 - core, core]).astype(jnp.int32)
    *early, last = size
    blocks, rows = [collect(p) for p in size], [low[p] for p in size]
    total = product(blocks[:-1], rows[:-1], (panels[0], panels[0]), sides, None, [[0], []])
    final = functools.partial(product, blocks, rows, panels)
    theirs = final(sides[:1], total, [[1], [0, 1]])
    swapped = send(theirs[0], flip_core)
    ours = final(sides[1:], total, [[1], [0, 1]])
    return ours[0] + swapped, gradient + token[0, 0]


def solution(mesh):
    fine = Mesh(mesh.devices.reshape(SIZES), NAMES)
    return jax.shard_map(
        body,
        mesh=fine,
        in_specs=(P(("x", "zlo"), ("zhi", "y", "core")), P(("x", "zlo")), P(), P(("x", "zlo"))),
        out_specs=(P(("x", "zlo"), ("zhi", "y", "core")), P(("zhi", "y", "core"))),
        check_vma=False,
    )
```

```python
import functools

import jax
import jax.numpy as jnp
from jax import lax
from jax.experimental import pallas as pl
from jax.experimental.pallas import tpu as pltpu
from jax.sharding import Mesh, PartitionSpec as P

NAMES = ("x", "zlo", "zhi", "y", "core")
SIZES = (4, 2, 2, 4, 2)
X, ZLO, ZHI, Y, CORE = SIZES
PHASES = (96, 128)
TILE = 8
ORDER = (
    ('X1',),
    ('T1a',),
    ('T2a', 'T1a'),
    ('T1b', 'T1a'),
    ('NOa', 'T2a'),
    ('ZHa', 'T2a'),
    ('Z', 'X1'),
    ('T2b', 'T1b'),
    ('X2', 'X1'),
    ('FOa', 'NOa'),
    ('NPa', 'ZHa'),
    ('ZHb', 'T2b'),
    ('NOb', 'T2b'),
    ('V1', 'Z'),
    ('FPa', 'NPa', 'FOa'),
    ('FOb', 'NOb', 'FPa', 'X2'),
    ('NPb', 'ZHb', 'V1'),
    ('V2', 'V1'),
    ('FPb', 'NPb', 'FOb'),
)


def linear(x, zlo, zhi, y, core):
    return (((x * ZLO + zlo) * ZHI + zhi) * Y + y) * CORE + core


def send(value, target):
    pairs = []
    for x in range(X):
        for zlo in range(ZLO):
            for zhi in range(ZHI):
                for y in range(Y):
                    for core in range(CORE):
                        there = target(x, zlo, zhi, y, core)
                        pairs.append((linear(x, zlo, zhi, y, core), linear(*there)))
    return lax.ppermute(value, NAMES, pairs)


NEAR, FAR = (1, 3), (3, 1)


def flip_x(masks):
    return lambda x, zlo, zhi, y, core: (x ^ masks[core], zlo, zhi, y, core)


def flip_y(masks):
    return lambda x, zlo, zhi, y, core: (x, zlo, zhi, y ^ masks[core], core)


def flip_zlo(x, zlo, zhi, y, core):
    return x, zlo ^ 1, zhi, y, core


def flip_zhi(x, zlo, zhi, y, core):
    return x, zlo, zhi ^ 1, y, core


def flip_core(x, zlo, zhi, y, core):
    return x, zlo, zhi, y, core ^ 1


def spread_yz(x, zlo, zhi, y, core):
    y = y ^ (2 * ((x & 1) ^ core) + zlo)
    return x, zlo ^ (y & 1), zhi ^ (x >> 1) ^ core, y, core


def spread_x(x, zlo, zhi, y, core):
    return x ^ (2 * (zhi ^ core) + ((y >> 1) ^ core)), zlo, zhi, y, core


def in_two(value):
    high = value.astype(jnp.bfloat16)
    return high, (value - high.astype(jnp.float32)).astype(jnp.bfloat16)


def dot(a, b):
    return lax.dot_general(a, b, (((0,), (0,)), ((), ())), preferred_element_type=jnp.float32)


def contract(left, right):
    left_high, left_low = in_two(left.reshape(-1, left.shape[-1]))
    right_high, right_low = in_two(right.reshape(-1, right.shape[-1]))
    return dot(left_high, right_high) + (dot(left_low, right_high) + dot(left_high, right_low))


def accumulate(low, steps, based, pick_ref, *refs):
    lefts, rights, outs = refs[: len(low)], refs[len(low) : len(low) + 2 * CORE * len(steps)], refs[-CORE:]
    step = pl.program_id(1)
    columns = outs[0].shape[-1]

    def add(i):
        named = steps[i][0]
        left = jnp.concatenate([lefts[k][0] for k in named], 1)
        first, last = low[named[0]], low[named[-1]] + lefts[named[-1]].shape[2]
        pairs = []
        for pair in range(2):
            at = 2 * CORE * i + CORE * pair
            pairs.append(jnp.concatenate([rights[at + side][:, first:last] for side in range(CORE)], 2))
        term = contract(left, jnp.concatenate(pairs, 0))
        for side, out_ref in enumerate(outs):
            part = term[:, side * columns : (side + 1) * columns]
            if based and i == 0:
                part = part + refs[len(low) + 2 * CORE * len(steps) + side][...]
            out_ref[...] = part if i == 0 else out_ref[...] + part

    for i in range(len(steps)):
        pl.when(step == i)(functools.partial(add, i))


def product(lefts, low, rights, sides, steps, base=()):
    columns = rights[0].shape[-1] // CORE
    rows, many = sum(left.shape[2] for left in lefts), len(steps)

    def left_spec(k, left):
        first = min(z for named, z in steps if k in named)
        return pl.BlockSpec(
            (1, X, left.shape[2], columns), lambda h, i, pick: (jnp.maximum(i, first), 0, 0, h)
        )

    def right_spec(right, side):
        return pl.BlockSpec((2, right.shape[1], columns), lambda h, i, pick: (0, 0, pick[side]))

    half = pl.BlockSpec((columns, columns), lambda h, i, pick: (h, 0))
    return pl.pallas_call(
        functools.partial(accumulate, low, steps, len(base) > 0),
        grid_spec=pltpu.PrefetchScalarGridSpec(
            num_scalar_prefetch=1,
            grid=(CORE, many),
            in_specs=[left_spec(k, left) for k, left in enumerate(lefts)]
            + [right_spec(right, side) for right in rights for side in range(CORE)]
            + [half] * len(base),
            out_specs=[half] * CORE,
        ),
        out_shape=[jax.ShapeDtypeStruct((CORE * columns, columns), jnp.float32)] * CORE,
        compiler_params=pltpu.CompilerParams(vmem_limit_bytes=61 * 2**20),
        cost_estimate=pl.CostEstimate(
            flops=48 * many * rows * CORE * columns * columns,
            bytes_accessed=64 * many * rows * columns,
            transcendentals=0,
        ),
    )(sides, *lefts, *(right for right in rights for _ in range(CORE)), *base)


def place(buffer, shape, blocks):
    out = jnp.zeros(shape, jnp.float32) if buffer is None else buffer
    for array, index, one, two in blocks:
        block = array if index is None else array[index]
        out = lax.dynamic_update_slice(out, block[None, None, : shape[2]], (one, two, 0, 0))
    return out


def body(jacobian, obs_group, group_weight, misfit):
    x, zlo, zhi, y, core = (lax.axis_index(name) for name in NAMES)
    count, columns = jacobian.shape[0] // CORE, jacobian.shape[1]
    levels = jnp.arange(group_weight.shape[0], dtype=jnp.int32)
    onehot = (obs_group[:, None] == levels[None, :]).astype(jnp.float32)
    weight_row = jnp.sum(onehot * group_weight[None, :], axis=1)
    names = "abcd"[: len(PHASES)]
    low = {p: sum(PHASES[: names.index(p)]) for p in names}
    size = dict(zip(names, PHASES))
    names_last = names[-1]
    got, sent = {}, {}

    kept = lax.dynamic_slice_in_dim(jacobian, core * count, count, 0)
    given = lax.dynamic_slice_in_dim(jacobian, (1 - core) * count, count, 0)
    taken = send(given, flip_core)
    mine = jnp.where(
        core == 0, jnp.concatenate([kept, taken], 1), jnp.concatenate([taken, kept], 1)
    )
    row_weight = lax.dynamic_slice_in_dim(weight_row, core * count, count, 0)[:, None]
    row_misfit = lax.dynamic_slice_in_dim(misfit, core * count, count, 0)[:, None]
    local = jnp.sum(mine * (row_weight * row_misfit), axis=0)

    def weighted(p):
        rows = slice(low[p], low[p] + size[p])
        return mine[rows] * row_weight[rows]

    def wide():
        return jnp.concatenate([mine, jnp.broadcast_to(local[None], (TILE, 2 * columns))], 0)

    def partner():
        return got["Z"].at[count:].add(local[None])

    def both(*names):
        return jnp.concatenate([got[n] if got[n].ndim == 3 else got[n][None] for n in names], 0)

    rings = {"N": flip_y(NEAR), "F": flip_y(FAR)}
    moves = {
        "X1": (lambda: mine, flip_x(NEAR)),
        "X2": (lambda: jnp.stack([mine, got["X1"]]), flip_x(FAR)),
        "Z": (wide, flip_zlo),
        "V1": (partner, flip_x(NEAR)),
        "V2": (lambda: jnp.stack([partner(), got["V1"]]), flip_x(FAR)),
    }
    for p in size:
        moves["T1" + p] = (functools.partial(weighted, p), spread_yz)
        moves["T2" + p] = (lambda p=p: got["T1" + p], spread_x)
        moves["ZH" + p] = (lambda p=p: got["T2" + p], flip_zhi)
        moves["NO" + p] = (lambda p=p: got["T2" + p], rings["N"])
        moves["FO" + p] = (lambda p=p: both("T2" + p, "NO" + p), rings["F"])
        moves["NP" + p] = (lambda p=p: got["ZH" + p], rings["N"])
        moves["FP" + p] = (lambda p=p: both("ZH" + p, "NP" + p), rings["F"])
        moves["NC" + p] = (lambda p=p: both("T2" + p, "ZH" + p), rings["N"])
        moves["FC" + p] = (lambda p=p: both("T2" + p, "ZH" + p, "NC" + p), rings["F"])

    token = jnp.zeros((TILE, 128), jnp.float32)
    for name, *after in ORDER:
        value = moves[name][0]()
        if after:
            held = [got[a] for a in after]
            value, token, *held = lax.optimization_barrier((value, token, *held))
            got.update(zip(after, held))
        sent[name] = value
        got[name] = send(value, moves[name][1])

    near = jnp.where(core == 0, NEAR[0], NEAR[1])
    far = jnp.where(core == 0, FAR[0], FAR[1])

    slope = sent["V1"][count] + got["V1"][count] + got["V2"][0, count] + got["V2"][1, count]
    gradient = lax.dynamic_slice_in_dim(slope, core * columns, columns, 0) + send(
        lax.dynamic_slice_in_dim(slope, (1 - core) * columns, columns, 0), flip_core
    )

    def collect(p):
        shape = (ZLO, X, size[p], 2 * columns)
        out = None
        for other, names in enumerate((("T2", "NO", "FO"), ("ZH", "NP", "FP"))):
            first, one, two = (got[n + p] for n in names)
            blocks = []
            for step, array, index in ((0, first, None), (near, one, None), (far, two, 0), (near ^ far, two, 1)):
                there = y ^ step
                high = zhi ^ other ^ core
                mixed = high ^ (there >> 1) ^ core
                blocks.append((array, index, there & 1, jnp.where(core == 0, 2 * high + mixed, 2 * mixed + high)))
            out = place(out, shape, blocks)
        return out

    sides = jnp.stack([1 - core, core]).astype(jnp.int32)
    sides, token, got["NPb"] = lax.optimization_barrier((sides, token, got["NPb"]))
    rows = [low[p] for p in size]
    first, late = collect("a"), collect("b")
    base = product([first], rows[:1], [sent["X2"], got["X2"]], sides, [([0], 0)])
    rights = [sent["X2"], got["X2"], sent["V2"], got["V2"]]
    steps = [([1], 0), ([0, 1], 1)]
    theirs, ours = product([first, late], rows, rights, sides, steps, base)
    return ours + send(theirs, flip_core), gradient + token[0, 0]


def solution(mesh):
    fine = Mesh(mesh.devices.reshape(SIZES), NAMES)
    return jax.shard_map(
        body,
        mesh=fine,
        in_specs=(P(("x", "zlo"), ("zhi", "y", "core")), P(("x", "zlo")), P(), P(("x", "zlo"))),
        out_specs=(P(("x", "zlo"), ("zhi", "y", "core")), P(("zhi", "y", "core"))),
        check_vma=False,
    )
```

```python
import functools

import jax
import jax.numpy as jnp
from jax import lax
from jax.experimental import pallas as pl
from jax.experimental.pallas import tpu as pltpu
from jax.sharding import Mesh, PartitionSpec as P

NAMES = ("x", "zlo", "zhi", "y", "core")
SIZES = (4, 2, 2, 4, 2)
X, ZLO, ZHI, Y, CORE = SIZES
PHASES = (96, 128)
TILE = 8
ORDER = (
    ('X1',),
    ('T1a',),
    ('T2a', 'T1a'),
    ('T1b', 'T1a'),
    ('NOa', 'T2a'),
    ('ZHa', 'T2a'),
    ('Z', 'X1'),
    ('T2b', 'T1b'),
    ('X2', 'X1'),
    ('FOa', 'NOa'),
    ('NPa', 'ZHa'),
    ('NOb', 'T2b'),
    ('ZHb', 'T2b'),
    ('FPa', 'NPa', 'FOa'),
    ('V1', 'Z'),
    ('FOb', 'NOb'),
    ('NPb', 'ZHb', 'FPa'),
    ('V2', 'V1', 'X2'),
    ('FPb', 'NPb', 'FOb'),
)


def linear(x, zlo, zhi, y, core):
    return (((x * ZLO + zlo) * ZHI + zhi) * Y + y) * CORE + core


def send(value, target):
    pairs = []
    for x in range(X):
        for zlo in range(ZLO):
            for zhi in range(ZHI):
                for y in range(Y):
                    for core in range(CORE):
                        there = target(x, zlo, zhi, y, core)
                        pairs.append((linear(x, zlo, zhi, y, core), linear(*there)))
    return lax.ppermute(value, NAMES, pairs)


NEAR, FAR = (1, 3), (3, 1)


def flip_x(masks):
    return lambda x, zlo, zhi, y, core: (x ^ masks[core], zlo, zhi, y, core)


def flip_y(masks):
    return lambda x, zlo, zhi, y, core: (x, zlo, zhi, y ^ masks[core], core)


def flip_zlo(x, zlo, zhi, y, core):
    return x, zlo ^ 1, zhi, y, core


def flip_zhi(x, zlo, zhi, y, core):
    return x, zlo, zhi ^ 1, y, core


def flip_core(x, zlo, zhi, y, core):
    return x, zlo, zhi, y, core ^ 1


def spread_yz(x, zlo, zhi, y, core):
    y = y ^ (2 * ((x & 1) ^ core) + zlo)
    return x, zlo ^ (y & 1), zhi ^ (x >> 1) ^ core, y, core


def spread_x(x, zlo, zhi, y, core):
    return x ^ (2 * (zhi ^ core) + ((y >> 1) ^ core)), zlo, zhi, y, core


def in_two(value):
    high = value.astype(jnp.bfloat16)
    return high, (value - high.astype(jnp.float32)).astype(jnp.bfloat16)


def dot(a, b):
    return lax.dot_general(a, b, (((0,), (0,)), ((), ())), preferred_element_type=jnp.float32)


def contract(left, right):
    left_high, left_low = in_two(left.reshape(-1, left.shape[-1]))
    right_high, right_low = in_two(right.reshape(-1, right.shape[-1]))
    return dot(
        jnp.concatenate([left_high, left_low, left_high], 0),
        jnp.concatenate([right_high, right_high, right_low], 0),
    )


def accumulate(low, steps, based, pick_ref, *refs):
    lefts, rights, outs = refs[: len(low)], refs[len(low) : len(low) + 2 * CORE * len(steps)], refs[-CORE:]
    step = pl.program_id(1)
    columns = outs[0].shape[-1]

    def add(i):
        named = steps[i][0]
        left = jnp.concatenate([lefts[k][0] for k in named], 1)
        first, last = low[named[0]], low[named[-1]] + lefts[named[-1]].shape[2]
        pairs = []
        for pair in range(2):
            at = 2 * CORE * i + CORE * pair
            pairs.append(jnp.concatenate([rights[at + side][:, first:last] for side in range(CORE)], 2))
        term = contract(left, jnp.concatenate(pairs, 0))
        for side, out_ref in enumerate(outs):
            part = term[:, side * columns : (side + 1) * columns]
            if based and i == 0:
                part = part + refs[len(low) + 2 * CORE * len(steps) + side][...]
            out_ref[...] = part if i == 0 else out_ref[...] + part

    for i in range(len(steps)):
        pl.when(step == i)(functools.partial(add, i))


def product(lefts, low, rights, sides, steps, base=()):
    columns = rights[0].shape[-1] // CORE
    rows, many = sum(left.shape[2] for left in lefts), len(steps)

    def left_spec(k, left):
        first = min(z for named, z in steps if k in named)
        return pl.BlockSpec(
            (1, X, left.shape[2], columns), lambda h, i, pick: (jnp.maximum(i, first), 0, 0, h)
        )

    def right_spec(right, side):
        return pl.BlockSpec((2, right.shape[1], columns), lambda h, i, pick: (0, 0, pick[side]))

    half = pl.BlockSpec((columns, columns), lambda h, i, pick: (h, 0))
    return pl.pallas_call(
        functools.partial(accumulate, low, steps, len(base) > 0),
        grid_spec=pltpu.PrefetchScalarGridSpec(
            num_scalar_prefetch=1,
            grid=(CORE, many),
            in_specs=[left_spec(k, left) for k, left in enumerate(lefts)]
            + [right_spec(right, side) for right in rights for side in range(CORE)]
            + [half] * len(base),
            out_specs=[half] * CORE,
        ),
        out_shape=[jax.ShapeDtypeStruct((CORE * columns, columns), jnp.float32)] * CORE,
        compiler_params=pltpu.CompilerParams(vmem_limit_bytes=61 * 2**20),
        cost_estimate=pl.CostEstimate(
            flops=48 * many * rows * CORE * columns * columns,
            bytes_accessed=64 * many * rows * columns,
            transcendentals=0,
        ),
    )(sides, *lefts, *(right for right in rights for _ in range(CORE)), *base)


def place(buffer, shape, blocks):
    out = jnp.zeros(shape, jnp.float32) if buffer is None else buffer
    for array, index, one, two in blocks:
        block = array if index is None else array[index]
        out = lax.dynamic_update_slice(out, block[None, None, : shape[2]], (one, two, 0, 0))
    return out


def body(jacobian, obs_group, group_weight, misfit):
    x, zlo, zhi, y, core = (lax.axis_index(name) for name in NAMES)
    count, columns = jacobian.shape[0] // CORE, jacobian.shape[1]
    levels = jnp.arange(group_weight.shape[0], dtype=jnp.int32)
    onehot = (obs_group[:, None] == levels[None, :]).astype(jnp.float32)
    weight_row = jnp.sum(onehot * group_weight[None, :], axis=1)
    names = "abcd"[: len(PHASES)]
    low = {p: sum(PHASES[: names.index(p)]) for p in names}
    size = dict(zip(names, PHASES))
    names_last = names[-1]
    got, sent = {}, {}

    kept = lax.dynamic_slice_in_dim(jacobian, core * count, count, 0)
    given = lax.dynamic_slice_in_dim(jacobian, (1 - core) * count, count, 0)
    taken = send(given, flip_core)
    mine = jnp.where(
        core == 0, jnp.concatenate([kept, taken], 1), jnp.concatenate([taken, kept], 1)
    )
    row_weight = lax.dynamic_slice_in_dim(weight_row, core * count, count, 0)[:, None]
    row_misfit = lax.dynamic_slice_in_dim(misfit, core * count, count, 0)[:, None]
    local = jnp.sum(mine * (row_weight * row_misfit), axis=0)

    def weighted(p):
        rows = slice(low[p], low[p] + size[p])
        return mine[rows] * row_weight[rows]

    def wide():
        return jnp.concatenate([mine, jnp.broadcast_to(local[None], (TILE, 2 * columns))], 0)

    def partner():
        return got["Z"].at[count:].add(local[None])

    def both(*names):
        return jnp.concatenate([got[n] if got[n].ndim == 3 else got[n][None] for n in names], 0)

    rings = {"N": flip_y(NEAR), "F": flip_y(FAR)}
    moves = {
        "X1": (lambda: mine, flip_x(NEAR)),
        "X2": (lambda: jnp.stack([mine, got["X1"]]), flip_x(FAR)),
        "Z": (wide, flip_zlo),
        "V1": (partner, flip_x(NEAR)),
        "V2": (lambda: jnp.stack([partner(), got["V1"]]), flip_x(FAR)),
    }
    for p in size:
        moves["T1" + p] = (functools.partial(weighted, p), spread_yz)
        moves["T2" + p] = (lambda p=p: got["T1" + p], spread_x)
        moves["ZH" + p] = (lambda p=p: got["T2" + p], flip_zhi)
        moves["NO" + p] = (lambda p=p: got["T2" + p], rings["N"])
        moves["FO" + p] = (lambda p=p: both("T2" + p, "NO" + p), rings["F"])
        moves["NP" + p] = (lambda p=p: got["ZH" + p], rings["N"])
        moves["FP" + p] = (lambda p=p: both("ZH" + p, "NP" + p), rings["F"])
        moves["NC" + p] = (lambda p=p: both("T2" + p, "ZH" + p), rings["N"])
        moves["FC" + p] = (lambda p=p: both("T2" + p, "ZH" + p, "NC" + p), rings["F"])

    token = jnp.zeros((TILE, 128), jnp.float32)
    for name, *after in ORDER:
        value = moves[name][0]()
        if after:
            held = [got[a] for a in after]
            value, token, *held = lax.optimization_barrier((value, token, *held))
            got.update(zip(after, held))
        sent[name] = value
        got[name] = send(value, moves[name][1])

    near = jnp.where(core == 0, NEAR[0], NEAR[1])
    far = jnp.where(core == 0, FAR[0], FAR[1])

    slope = sent["V1"][count] + got["V1"][count] + got["V2"][0, count] + got["V2"][1, count]
    gradient = lax.dynamic_slice_in_dim(slope, core * columns, columns, 0) + send(
        lax.dynamic_slice_in_dim(slope, (1 - core) * columns, columns, 0), flip_core
    )

    def collect(p):
        shape = (ZLO, X, size[p], 2 * columns)
        out = None
        for other, names in enumerate((("T2", "NO", "FO"), ("ZH", "NP", "FP"))):
            first, one, two = (got[n + p] for n in names)
            blocks = []
            for step, array, index in ((0, first, None), (near, one, None), (far, two, 0), (near ^ far, two, 1)):
                there = y ^ step
                high = zhi ^ other ^ core
                mixed = high ^ (there >> 1) ^ core
                blocks.append((array, index, there & 1, jnp.where(core == 0, 2 * high + mixed, 2 * mixed + high)))
            out = place(out, shape, blocks)
        return out

    sides = jnp.stack([1 - core, core]).astype(jnp.int32)
    sides, token, got["NPb"] = lax.optimization_barrier((sides, token, got["NPb"]))
    rows = [low[p] for p in size]
    first, late = collect("a"), collect("b")
    base = product([first], rows[:1], [sent["X2"], got["X2"]], sides, [([0], 0)])
    rights = [sent["X2"], got["X2"], sent["V2"], got["V2"]]
    steps = [([1], 0), ([0, 1], 1)]
    theirs, ours = product([first, late], rows, rights, sides, steps, base)
    return ours + send(theirs, flip_core), gradient + token[0, 0]


def solution(mesh):
    fine = Mesh(mesh.devices.reshape(SIZES), NAMES)
    return jax.shard_map(
        body,
        mesh=fine,
        in_specs=(P(("x", "zlo"), ("zhi", "y", "core")), P(("x", "zlo")), P(), P(("x", "zlo"))),
        out_specs=(P(("x", "zlo"), ("zhi", "y", "core")), P(("zhi", "y", "core"))),
        check_vma=False,
    )
```

```python
import functools

import jax
import jax.numpy as jnp
from jax import lax
from jax.experimental import pallas as pl
from jax.experimental.pallas import tpu as pltpu
from jax.sharding import Mesh, PartitionSpec as P

NAMES = ("x", "zlo", "zhi", "y", "core")
SIZES = (4, 2, 2, 4, 2)
X, ZLO, ZHI, Y, CORE = SIZES
PHASES = (96, 128)
TILE = 8
ORDER = (
    ('X1',),
    ('T1a',),
    ('T2a', 'T1a'),
    ('T1b', 'T1a'),
    ('NOa', 'T2a'),
    ('ZHa', 'T2a'),
    ('Z', 'X1'),
    ('T2b', 'T1b'),
    ('X2', 'X1'),
    ('FOa', 'NOa'),
    ('NPa', 'ZHa'),
    ('NOb', 'T2b'),
    ('ZHb', 'T2b'),
    ('FPa', 'NPa', 'FOa'),
    ('V1', 'Z'),
    ('FOb', 'NOb'),
    ('NPb', 'ZHb', 'FPa'),
    ('V2', 'V1', 'X2'),
    ('FPb', 'NPb', 'FOb'),
)


def linear(x, zlo, zhi, y, core):
    return (((x * ZLO + zlo) * ZHI + zhi) * Y + y) * CORE + core


def send(value, target):
    pairs = []
    for x in range(X):
        for zlo in range(ZLO):
            for zhi in range(ZHI):
                for y in range(Y):
                    for core in range(CORE):
                        there = target(x, zlo, zhi, y, core)
                        pairs.append((linear(x, zlo, zhi, y, core), linear(*there)))
    return lax.ppermute(value, NAMES, pairs)


NEAR, FAR = (1, 3), (3, 1)


def flip_x(masks):
    return lambda x, zlo, zhi, y, core: (x ^ masks[core], zlo, zhi, y, core)


def flip_y(masks):
    return lambda x, zlo, zhi, y, core: (x, zlo, zhi, y ^ masks[core], core)


def flip_zlo(x, zlo, zhi, y, core):
    return x, zlo ^ 1, zhi, y, core


def flip_zhi(x, zlo, zhi, y, core):
    return x, zlo, zhi ^ 1, y, core


def flip_core(x, zlo, zhi, y, core):
    return x, zlo, zhi, y, core ^ 1


def spread_yz(x, zlo, zhi, y, core):
    y = y ^ (2 * ((x & 1) ^ core) + zlo)
    return x, zlo ^ (y & 1), zhi ^ (x >> 1) ^ core, y, core


def spread_x(x, zlo, zhi, y, core):
    return x ^ (2 * (zhi ^ core) + ((y >> 1) ^ core)), zlo, zhi, y, core


def in_two(value):
    high = value.astype(jnp.bfloat16)
    return high, (value - high.astype(jnp.float32)).astype(jnp.bfloat16)


def dot(a, b):
    return lax.dot_general(a, b, (((0,), (0,)), ((), ())), preferred_element_type=jnp.float32)


def contract(left, right):
    left_high, left_low = in_two(left.reshape(-1, left.shape[-1]))
    right_high, right_low = in_two(right.reshape(-1, right.shape[-1]))
    return dot(
        jnp.concatenate([left_high, left_low, left_high], 0),
        jnp.concatenate([right_high, right_high, right_low], 0),
    )


def accumulate(low, steps, based, many_sides, pick_ref, *refs):
    lefts, rights, outs = refs[: len(low)], refs[len(low) : len(low) + 2 * many_sides * len(steps)], refs[-many_sides:]
    step = pl.program_id(1)
    columns = outs[0].shape[-1]

    def add(i):
        named = steps[i][0]
        left = jnp.concatenate([lefts[k][0] for k in named], 1)
        first, last = low[named[0]], low[named[-1]] + lefts[named[-1]].shape[2]
        pairs = []
        for pair in range(2):
            at = 2 * many_sides * i + many_sides * pair
            pairs.append(jnp.concatenate([rights[at + side][:, first:last] for side in range(many_sides)], 2))
        term = contract(left, jnp.concatenate(pairs, 0))
        for side, out_ref in enumerate(outs):
            part = term[:, side * columns : (side + 1) * columns]
            if based and i == 0:
                part = part + refs[len(low) + 2 * many_sides * len(steps) + side][...]
            out_ref[...] = part if i == 0 else out_ref[...] + part

    for i in range(len(steps)):
        pl.when(step == i)(functools.partial(add, i))


def product(lefts, low, rights, sides, steps, base=()):
    columns = rights[0].shape[-1] // CORE
    many_sides = sides.shape[0]
    rows, many = sum(left.shape[2] for left in lefts), len(steps)

    def left_spec(k, left):
        first = min(z for named, z in steps if k in named)
        return pl.BlockSpec(
            (1, X, left.shape[2], columns), lambda h, i, pick: (jnp.maximum(i, first), 0, 0, h)
        )

    def right_spec(right, side):
        return pl.BlockSpec((2, right.shape[1], columns), lambda h, i, pick: (0, 0, pick[side]))

    half = pl.BlockSpec((columns, columns), lambda h, i, pick: (h, 0))
    return pl.pallas_call(
        functools.partial(accumulate, low, steps, len(base) > 0, many_sides),
        grid_spec=pltpu.PrefetchScalarGridSpec(
            num_scalar_prefetch=1,
            grid=(CORE, many),
            in_specs=[left_spec(k, left) for k, left in enumerate(lefts)]
            + [right_spec(right, side) for right in rights for side in range(many_sides)]
            + [half] * len(base),
            out_specs=[half] * many_sides,
        ),
        out_shape=[jax.ShapeDtypeStruct((CORE * columns, columns), jnp.float32)] * many_sides,
        compiler_params=pltpu.CompilerParams(vmem_limit_bytes=61 * 2**20),
        cost_estimate=pl.CostEstimate(
            flops=48 * many * rows * CORE * columns * columns,
            bytes_accessed=64 * many * rows * columns,
            transcendentals=0,
        ),
    )(sides, *lefts, *(right for right in rights for _ in range(many_sides)), *base)


def place(buffer, shape, blocks):
    out = jnp.zeros(shape, jnp.float32) if buffer is None else buffer
    for array, index, one, two in blocks:
        block = array if index is None else array[index]
        out = lax.dynamic_update_slice(out, block[None, None, : shape[2]], (one, two, 0, 0))
    return out


def body(jacobian, obs_group, group_weight, misfit):
    x, zlo, zhi, y, core = (lax.axis_index(name) for name in NAMES)
    count, columns = jacobian.shape[0] // CORE, jacobian.shape[1]
    levels = jnp.arange(group_weight.shape[0], dtype=jnp.int32)
    onehot = (obs_group[:, None] == levels[None, :]).astype(jnp.float32)
    weight_row = jnp.sum(onehot * group_weight[None, :], axis=1)
    names = "abcd"[: len(PHASES)]
    low = {p: sum(PHASES[: names.index(p)]) for p in names}
    size = dict(zip(names, PHASES))
    names_last = names[-1]
    got, sent = {}, {}

    kept = lax.dynamic_slice_in_dim(jacobian, core * count, count, 0)
    given = lax.dynamic_slice_in_dim(jacobian, (1 - core) * count, count, 0)
    taken = send(given, flip_core)
    mine = jnp.where(
        core == 0, jnp.concatenate([kept, taken], 1), jnp.concatenate([taken, kept], 1)
    )
    row_weight = lax.dynamic_slice_in_dim(weight_row, core * count, count, 0)[:, None]
    row_misfit = lax.dynamic_slice_in_dim(misfit, core * count, count, 0)[:, None]
    local = jnp.sum(mine * (row_weight * row_misfit), axis=0)

    def weighted(p):
        rows = slice(low[p], low[p] + size[p])
        return mine[rows] * row_weight[rows]

    def wide():
        return jnp.concatenate([mine, jnp.broadcast_to(local[None], (TILE, 2 * columns))], 0)

    def partner():
        return got["Z"].at[count:].add(local[None])

    def both(*names):
        return jnp.concatenate([got[n] if got[n].ndim == 3 else got[n][None] for n in names], 0)

    rings = {"N": flip_y(NEAR), "F": flip_y(FAR)}
    moves = {
        "X1": (lambda: mine, flip_x(NEAR)),
        "X2": (lambda: jnp.stack([mine, got["X1"]]), flip_x(FAR)),
        "Z": (wide, flip_zlo),
        "V1": (partner, flip_x(NEAR)),
        "V2": (lambda: jnp.stack([partner(), got["V1"]]), flip_x(FAR)),
    }
    for p in size:
        moves["T1" + p] = (functools.partial(weighted, p), spread_yz)
        moves["T2" + p] = (lambda p=p: got["T1" + p], spread_x)
        moves["ZH" + p] = (lambda p=p: got["T2" + p], flip_zhi)
        moves["NO" + p] = (lambda p=p: got["T2" + p], rings["N"])
        moves["FO" + p] = (lambda p=p: both("T2" + p, "NO" + p), rings["F"])
        moves["NP" + p] = (lambda p=p: got["ZH" + p], rings["N"])
        moves["FP" + p] = (lambda p=p: both("ZH" + p, "NP" + p), rings["F"])
        moves["NC" + p] = (lambda p=p: both("T2" + p, "ZH" + p), rings["N"])
        moves["FC" + p] = (lambda p=p: both("T2" + p, "ZH" + p, "NC" + p), rings["F"])

    token = jnp.zeros((TILE, 128), jnp.float32)
    for name, *after in ORDER:
        value = moves[name][0]()
        if after:
            held = [got[a] for a in after]
            value, token, *held = lax.optimization_barrier((value, token, *held))
            got.update(zip(after, held))
        sent[name] = value
        got[name] = send(value, moves[name][1])

    near = jnp.where(core == 0, NEAR[0], NEAR[1])
    far = jnp.where(core == 0, FAR[0], FAR[1])

    slope = sent["V1"][count] + got["V1"][count] + got["V2"][0, count] + got["V2"][1, count]
    gradient = lax.dynamic_slice_in_dim(slope, core * columns, columns, 0) + send(
        lax.dynamic_slice_in_dim(slope, (1 - core) * columns, columns, 0), flip_core
    )

    def collect(p):
        shape = (ZLO, X, size[p], 2 * columns)
        out = None
        for other, names in enumerate((("T2", "NO", "FO"), ("ZH", "NP", "FP"))):
            first, one, two = (got[n + p] for n in names)
            blocks = []
            for step, array, index in ((0, first, None), (near, one, None), (far, two, 0), (near ^ far, two, 1)):
                there = y ^ step
                high = zhi ^ other ^ core
                mixed = high ^ (there >> 1) ^ core
                blocks.append((array, index, there & 1, jnp.where(core == 0, 2 * high + mixed, 2 * mixed + high)))
            out = place(out, shape, blocks)
        return out

    sides = jnp.stack([1 - core, core]).astype(jnp.int32)
    sides, token, got["NPb"] = lax.optimization_barrier((sides, token, got["NPb"]))
    rows = [low[p] for p in size]
    first, late = collect("a"), collect("b")
    base = product([first], rows[:1], [sent["X2"], got["X2"]], sides, [([0], 0)])
    rights = [sent["X2"], got["X2"], sent["V2"], got["V2"]]
    steps = [([1], 0), ([0, 1], 1)]
    (theirs,) = product([first, late], rows, rights, sides[:1], steps, base[:1])
    swapped = send(theirs, flip_core)
    (ours,) = product([first, late], rows, rights, sides[1:], steps, base[1:])
    return ours + swapped, gradient + token[0, 0]


def solution(mesh):
    fine = Mesh(mesh.devices.reshape(SIZES), NAMES)
    return jax.shard_map(
        body,
        mesh=fine,
        in_specs=(P(("x", "zlo"), ("zhi", "y", "core")), P(("x", "zlo")), P(), P(("x", "zlo"))),
        out_specs=(P(("x", "zlo"), ("zhi", "y", "core")), P(("zhi", "y", "core"))),
        check_vma=False,
    )
```
